32 devices in a mesh: dp: 8 (over z, y), expert: 4 (over x, core).
Axes of the slice: x: 2, y: 2, z: 4, core: 2. Of those that a mesh axis runs over, the one named last changes fastest.
Arguments:
- tokens: bfloat16 [4096, 2048], P(('dp', 'expert')), may hold values from -6 to 6
- expert_ids: int32 [4096, 2], P(('dp', 'expert')), may hold values from 0 to 3, all different within a row; in each aligned block of 128 rows (0 to 127, 128 to 255, ...) at most 96 rows name the same one
- gates: float32 [4096, 2], P(('dp', 'expert')), may hold values from 0.2 to 1
- w_in: bfloat16 [4, 2048, 1536], P('expert'), may hold values from -0.125 to 0.125
- w_out: bfloat16 [4, 768, 2048], P('expert'), may hold values from -0.21875 to 0.21875
- out_grad: bfloat16 [4096, 2048], P(('dp', 'expert')), may hold values from -6 to 6
Outputs:
- mixed: bfloat16 [4096, 2048], P(('dp', 'expert'))
- token_grad: bfloat16 [4096, 2048], P(('dp', 'expert'))
- gate_grad: float32 [4096, 2], P(('dp', 'expert'))
- w_in_grad: bfloat16 [4, 2048, 1536], P('expert', 'dp')
- w_out_grad: bfloat16 [4, 768, 2048], P('expert', 'dp')
The draws below stay inside these ranges and needn't reach their ends.
Inputs may be any that keep to these rules, and one draw needn't show every extreme that they name: `expert_ids`: the 2 ids of a token differ. Among the 128 tokens of one device no expert is named more than 96 times, and in every draw some expert is named exactly 96 times by the tokens of some device.
All inputs are finite; a program needn't handle non-finite values.
Results may differ from the reference program's by a relative error of at most 0.0065.
Values may be sent and summed in bfloat16 or wider, within the bound.
A program may use at most 128 MiB of HBM per device.

```python
import math
import jax
import jax.numpy as jnp
import numpy as np
from jax import lax

D = 2048
FF = 768
TOP = 2
TOK_DEV = 128
EXPERTS = 4
CAP = 96
TOKENS = 4096


def strengthened(entries, own_key, source, target, shards_of, factor):
    def block_of(position):
        return (jnp.arange(entries.shape[position]) // (entries.shape[position] // shards_of)).reshape((-1,) + (1,) * (entries.ndim - 1 - position))

    first = jax.random.permutation(own_key, shards_of)[block_of(target)]
    far = (block_of(target) + shards_of // 2) % shards_of
    return jnp.where((block_of(source) == first) | (block_of(source) == far), factor * entries, entries)


def levels(stream_key, dims, split, smallest, high):
    loudness, own = 1.0, jax.random.fold_in(stream_key, 6)
    for dim, blocks in split:
        heights = jnp.exp(jax.random.uniform(jax.random.fold_in(own, dim), (blocks,), jnp.float32, smallest / len(split), high / len(split)))
        loudness = loudness * jnp.repeat(heights, dims[dim] // blocks).reshape([-1 if axis == dim else 1 for axis in range(len(dims))])
    return loudness


def deal_out(stream_key, own, number, rows, number_of, top, most, skew):
    sequence = jax.random.permutation(stream_key, number_of)
    heavy_load, usual = shares(number_of, rows * top, most, skew, True), shares(number_of, rows * top, most, skew, False)
    places = jnp.arange(number_of)

    def named(lengths, rotation):
        used = int((lengths > 0).sum())
        fixed = max(1, used // 4)
        passed = fixed + (places - fixed + rotation * (used - fixed)) % max(1, number_of - fixed)
        return jnp.zeros((number_of,), jnp.int32).at[sequence[jnp.where(places < fixed, places, passed)]].set(jnp.asarray(lengths, jnp.int32))

    lengths = jnp.where(number % 4 == 0, named(heavy_load, number // 4), named(usual, number - number // 4 - 1))
    mixed = jax.random.permutation(jax.random.fold_in(own, 3), number_of)
    source_of, receiver = mixed[0:number_of // 2 * 2:2], mixed[1:number_of // 2 * 2:2]
    margin = jnp.minimum(lengths[source_of] - 1, most - lengths[receiver]) // 2
    margin = jnp.where((source_of == sequence[0]) | (receiver == sequence[0]) | (lengths[receiver] == 0), 0, jnp.maximum(margin, 0))
    passed = jax.random.randint(jax.random.fold_in(own, 4), (number_of // 2,), 0, 1 << 20) % (margin + 1)
    lengths = lengths.at[source_of].add(-passed).at[receiver].add(passed)
    members = jnp.searchsorted(jnp.cumsum(lengths), jnp.arange(rows * top), side="right").astype(jnp.int32)
    grid = members.reshape(top, rows).T
    grid = grid[jax.random.permutation(jax.random.fold_in(own, 1), rows)]
    rotation = jax.random.randint(jax.random.fold_in(own, 2), (rows, 1), 0, top)
    return jnp.take_along_axis(grid, (jnp.arange(top)[None, :] + rotation) % top, axis=1)


def shares(number_of, total, limit, slope, full):
    loads = [(1 << 20) // math.isqrt(standing ** slope) + 1 for standing in range(1, number_of + 1)]
    largest = limit if full else min(limit, max(-(-total // number_of), total * loads[0] // sum(loads)))
    least = 1 if total - largest >= number_of - 1 else 0
    given, spare = [largest] + [least] * (number_of - 1), total - largest - least * (number_of - 1)
    while spare > 0:
        candidates = [i for i in range(1, number_of) if given[i] < largest] or [i for i in range(1, number_of) if given[i] < limit]
        whole, left = sum([loads[i] for i in candidates]), spare
        for i in candidates:
            extra = min(limit - given[i], max(1, left * loads[i] // whole), spare)
            given[i] = given[i] + extra
            spare = spare - extra
    return np.array(given)


def gaussian(own_key, dims, width, limit, shards=(), kind=jnp.bfloat16):
    drawn = width * jax.random.normal(own_key, dims, jnp.float32)
    if shards:
        drawn = drawn * levels(own_key, dims, shards, -0.22, 0.18)
    return jnp.clip(drawn, -limit, limit).astype(kind)


def bell_draw_with(stream_key, extent, width, bound, pieces, heavy, kind=jnp.bfloat16):
    entries = width * jax.random.normal(stream_key, extent, jnp.float32)
    if pieces:
        entries = entries * levels(stream_key, extent, pieces, -0.22, 0.18)
    return jnp.clip(strengthened(entries, jax.random.fold_in(stream_key, 3), *heavy), -bound, bound).astype(kind)


def setup_inputs(seed: int = 0) -> dict:
    streams_of = jax.random.split(jax.random.key(seed), 7)
    tokens = bell_draw_with(streams_of[0], (TOKENS, D), 1.0, 6.0, ((0, 32),), (0, 1, 32, 2.75))
    expert_ids_keys = jax.random.split(jax.random.fold_in(streams_of[1], 1), TOKENS // TOK_DEV)
    expert_ids_turns = jax.random.permutation(jax.random.fold_in(streams_of[1], 3), TOKENS // TOK_DEV)
    expert_ids = jax.vmap(lambda own, number: deal_out(jax.random.fold_in(streams_of[1], 2), own, number, TOK_DEV, EXPERTS, TOP, CAP, 2))(expert_ids_keys, expert_ids_turns).reshape((TOKENS, TOP))
    gates = jnp.clip(jnp.exp(math.log(1.0) - 1.609438 * jax.random.uniform(streams_of[2], (TOKENS, TOP), jnp.float32) ** levels(streams_of[2], (TOKENS, TOP), ((0, 32),), -0.2, 0.2)), 0.2, 1.0)
    w_in = gaussian(streams_of[3], (EXPERTS, D, 2 * FF), D ** -0.5, 0.125, ((0, 4),))
    w_out = gaussian(streams_of[4], (EXPERTS, FF, D), FF ** -0.5, 0.21875, ((0, 4),))
    out_grad = gaussian(streams_of[5], (TOKENS, D), 1.0, 6.0, ((0, 32),))
    return {"tokens": tokens, "expert_ids": expert_ids, "gates": gates, "w_in": w_in, "w_out": w_out, "out_grad": out_grad}


def swiglu_forward(gate_up, hidden_width):
    gate_part = gate_up[:, :hidden_width]
    up_part = gate_up[:, hidden_width:]
    return gate_part, up_part, (jax.nn.silu(gate_part) * up_part).astype(jnp.bfloat16)


def swiglu_backward(grad_hidden, gate_part, up_part):
    sigmoid_gate = jax.nn.sigmoid(gate_part)
    silu_gate = gate_part * sigmoid_gate
    grad_gate = grad_hidden * up_part * (sigmoid_gate * (1.0 + gate_part * (1.0 - sigmoid_gate)))
    grad_up = grad_hidden * silu_gate
    return jnp.concatenate([grad_gate, grad_up], axis=1).astype(jnp.bfloat16)


def reference(tokens, expert_ids, gates, w_in, w_out, out_grad):
    entry_count = TOKENS * TOP
    slot_count = CAP * (TOKENS // TOK_DEV)
    flat_ids = expert_ids.reshape(entry_count)
    flat_gates = gates.reshape(entry_count)

    def per_expert(running, inputs):
        mixed_acc, grad_acc, gate_acc = running
        expert, weight_in, weight_out = inputs
        (positions,) = jnp.nonzero(flat_ids == expert, size=slot_count, fill_value=entry_count)
        positions = positions.astype(jnp.int32)
        is_valid = positions < entry_count
        token_rows = jnp.minimum(positions // TOP, TOKENS - 1).astype(jnp.int32)
        picked = jnp.where(is_valid[:, None], tokens[token_rows], jnp.zeros((), tokens.dtype))
        gate_up = jnp.dot(picked, weight_in, preferred_element_type=jnp.float32)
        gate_part, up_part, hidden = swiglu_forward(gate_up, FF)
        outputs = jnp.dot(hidden, weight_out, preferred_element_type=jnp.float32).astype(jnp.bfloat16)
        outputs_wide = outputs.astype(jnp.float32)
        row_gates = jnp.where(is_valid, flat_gates[jnp.minimum(positions, entry_count - 1)], jnp.zeros((), jnp.float32))
        upstream = out_grad[token_rows].astype(jnp.float32)
        mixed_acc = mixed_acc.at[token_rows].add(jnp.where(is_valid[:, None], row_gates[:, None] * outputs_wide, 0.0))
        gate_vals = jnp.sum(outputs_wide * upstream, axis=1)
        gate_acc = gate_acc.at[positions].set(gate_vals, mode="drop")
        grad_out = (row_gates[:, None] * upstream).astype(jnp.bfloat16)
        grad_hidden = jnp.dot(grad_out, weight_out.T, preferred_element_type=jnp.float32)
        grad_gate_up = swiglu_backward(grad_hidden, gate_part, up_part)
        grad_entry = jnp.dot(grad_gate_up, weight_in.T, preferred_element_type=jnp.float32).astype(jnp.bfloat16)
        grad_acc = grad_acc.at[token_rows].add(jnp.where(is_valid[:, None], grad_entry.astype(jnp.float32), 0.0))
        grad_w_out = jnp.dot(hidden.T, grad_out, preferred_element_type=jnp.float32)
        grad_w_in = jnp.dot(picked.T, grad_gate_up, preferred_element_type=jnp.float32)
        return (mixed_acc, grad_acc, gate_acc), (grad_w_in.astype(jnp.bfloat16), grad_w_out.astype(jnp.bfloat16))

    start = (jnp.zeros((TOKENS, D), jnp.float32), jnp.zeros((TOKENS, D), jnp.float32), jnp.zeros((entry_count,), jnp.float32))
    final, stacked = lax.scan(per_expert, start, (jnp.arange(EXPERTS, dtype=jnp.int32), w_in, w_out))
    mixed_acc, grad_acc, gate_acc = final
    return mixed_acc.astype(jnp.bfloat16), grad_acc.astype(jnp.bfloat16), gate_acc.reshape(TOKENS, TOP), stacked[0], stacked[1]
```

```python
import jax
import jax.numpy as jnp
from jax import lax
from jax.sharding import PartitionSpec as P


def swiglu_forward(gate_up, hidden_width):
    gate_part = gate_up[:, :hidden_width]
    up_part = gate_up[:, hidden_width:]
    return (gate_part, up_part, (jax.nn.silu(gate_part) * up_part).astype(jnp.bfloat16))


def swiglu_backward(grad_hidden, gate_part, up_part):
    sigmoid_gate = jax.nn.sigmoid(gate_part)
    silu_gate = gate_part * sigmoid_gate
    grad_gate = grad_hidden * up_part * (sigmoid_gate * (1.0 + gate_part * (1.0 - sigmoid_gate)))
    grad_up = grad_hidden * silu_gate
    return jnp.concatenate([grad_gate, grad_up], axis=1).astype(jnp.bfloat16)


def per_device(tokens, expert_ids, gates, w_in, w_out, out_grad):
    groups = lax.axis_size("expert")
    my_group = lax.axis_index("expert")
    token_rows, model_width = tokens.shape
    top_count = expert_ids.shape[1]
    hidden_width = w_out.shape[1]
    capacity = 3 * token_rows * top_count // (2 * groups)
    entries = token_rows * top_count
    flat_ids = expert_ids.reshape(entries)
    one_hot = (flat_ids[:, None] == jnp.arange(groups, dtype=jnp.int32)[None, :]).astype(jnp.int32)
    slot_rank = jnp.sum((jnp.cumsum(one_hot, axis=0) - one_hot) * one_hot, axis=1)
    dest_slot = flat_ids * capacity + slot_rank
    source_entry = (
        jnp.full((groups * capacity,), entries, jnp.int32)
        .at[dest_slot]
        .set(jnp.arange(entries, dtype=jnp.int32))
    )
    filled = source_entry < entries
    clamped_entry = jnp.minimum(source_entry, entries - 1)
    weight_in = w_in[0]
    weight_out = w_out[0]
    zero_value = jnp.zeros((), jnp.bfloat16)
    group_tok, group_ids = (
        lax.all_gather(tokens, "expert", axis=0, tiled=True),
        lax.all_gather(expert_ids.astype(jnp.bfloat16), "expert", axis=0, tiled=True),
    )
    ids_by_source = group_ids.astype(jnp.int32).reshape(groups, entries)
    is_mine = (ids_by_source == my_group).astype(jnp.int32)
    my_ranks = jnp.cumsum(is_mine, axis=1) - is_mine
    my_slots = jnp.where(is_mine > 0, my_ranks, capacity)
    source_index = jnp.broadcast_to(jnp.arange(groups, dtype=jnp.int32)[:, None], (groups, entries))
    entry_index = jnp.broadcast_to(jnp.arange(entries, dtype=jnp.int32)[None, :], (groups, entries))
    picked_entry = (
        jnp.full((groups, capacity), entries, jnp.int32)
        .at[source_index, my_slots]
        .set(entry_index, mode="drop")
    )
    picked_valid = picked_entry < entries
    picked_rows = (
        jnp.arange(groups, dtype=jnp.int32)[:, None] * token_rows
        + jnp.minimum(picked_entry, entries - 1) // top_count
    )
    received = jnp.where(picked_valid[..., None], group_tok[picked_rows], zero_value)
    received = received.reshape(groups * capacity, model_width)
    gate_up = jnp.dot(received, weight_in, preferred_element_type=jnp.float32)
    gate_part, up_part, hidden = swiglu_forward(gate_up, hidden_width)
    expert_out = jnp.dot(hidden, weight_out, preferred_element_type=jnp.float32).astype(
        jnp.bfloat16
    )
    returned = lax.all_to_all(
        expert_out.reshape(groups, capacity, model_width),
        "expert",
        split_axis=0,
        concat_axis=0,
        tiled=True,
    )
    returned = returned.reshape(groups * capacity, model_width)
    per_entry = returned[dest_slot].reshape(token_rows, top_count, model_width).astype(jnp.float32)
    upstream = out_grad.astype(jnp.float32)
    mixed = jnp.sum(gates[:, :, None] * per_entry, axis=1).astype(jnp.bfloat16)
    gate_grad = jnp.sum(per_entry * upstream[:, None, :], axis=2)
    grad_entries = (
        (gates[:, :, None] * upstream[:, None, :])
        .astype(jnp.bfloat16)
        .reshape(entries, model_width)
    )
    send_grads = jnp.where(filled[:, None], grad_entries[clamped_entry], zero_value)
    grad_rows = lax.all_to_all(
        send_grads.reshape(groups, capacity, model_width),
        "expert",
        split_axis=0,
        concat_axis=0,
        tiled=True,
    )
    grad_rows = grad_rows.reshape(groups * capacity, model_width)
    grad_hidden = jnp.dot(grad_rows, weight_out.T, preferred_element_type=jnp.float32)
    grad_gate_up = swiglu_backward(grad_hidden, gate_part, up_part)
    grad_inputs = jnp.dot(grad_gate_up, weight_in.T, preferred_element_type=jnp.float32).astype(
        jnp.bfloat16
    )
    grad_back = lax.all_to_all(
        grad_inputs.reshape(groups, capacity, model_width),
        "expert",
        split_axis=0,
        concat_axis=0,
        tiled=True,
    )
    grad_back = grad_back.reshape(groups * capacity, model_width)
    token_grad = jnp.sum(
        grad_back[dest_slot].reshape(token_rows, top_count, model_width).astype(jnp.float32), axis=1
    ).astype(jnp.bfloat16)
    grad_w_out = jnp.dot(hidden.T, grad_rows, preferred_element_type=jnp.float32)
    grad_w_in = jnp.dot(received.T, grad_gate_up, preferred_element_type=jnp.float32)
    shard_in, shard_out = (
        lax.psum_scatter(grad_w_in.astype(jnp.bfloat16)[None], "dp", scatter_dimension=1, tiled=True),
        lax.psum_scatter(grad_w_out.astype(jnp.bfloat16)[None], "dp", scatter_dimension=1, tiled=True),
    )
    return (
        mixed,
        token_grad,
        gate_grad,
        shard_in.astype(jnp.bfloat16),
        shard_out.astype(jnp.bfloat16),
    )


def solution(mesh):
    placed = (
        P(("dp", "expert"), None),
        P(("dp", "expert"), None),
        P(("dp", "expert"), None),
        P("expert", None, None),
        P("expert", None, None),
        P(("dp", "expert"), None),
    )
    return jax.shard_map(
        per_device,
        mesh=mesh,
        in_specs=placed,
        out_specs=(
            P(("dp", "expert"), None),
            P(("dp", "expert"), None),
            P(("dp", "expert"), None),
            P("expert", "dp", None),
            P("expert", "dp", None),
        ),
        check_vma=False,
    )
```

```python
import jax
import jax.numpy as jnp
from jax import lax
from jax.sharding import PartitionSpec as P


def swiglu_forward(gate_up, hidden_width):
    gate_part = gate_up[:, :hidden_width]
    up_part = gate_up[:, hidden_width:]
    return (gate_part, up_part, (jax.nn.silu(gate_part) * up_part).astype(jnp.bfloat16))


def swiglu_backward(grad_hidden, gate_part, up_part):
    sigmoid_gate = jax.nn.sigmoid(gate_part)
    silu_gate = gate_part * sigmoid_gate
    grad_gate = grad_hidden * up_part * (sigmoid_gate * (1.0 + gate_part * (1.0 - sigmoid_gate)))
    grad_up = grad_hidden * silu_gate
    return jnp.concatenate([grad_gate, grad_up], axis=1).astype(jnp.bfloat16)


def halving_sum(parts, axis):
    count = lax.axis_size(axis)
    me = lax.axis_index(axis)
    bit = 1
    while bit < count:
        mine = (me // bit) % 2
        pairs = parts.reshape((parts.shape[0] // 2, 2) + parts.shape[1:])
        keep = lax.dynamic_index_in_dim(pairs, mine, axis=1, keepdims=False)
        send = lax.dynamic_index_in_dim(pairs, 1 - mine, axis=1, keepdims=False)
        came = lax.ppermute(
            send.astype(jnp.bfloat16), axis, [(i, i ^ bit) for i in range(count)]
        )
        parts = keep.astype(jnp.float32) + came.astype(jnp.float32)
        bit *= 2
    return parts[0].astype(jnp.bfloat16)


def per_device(tokens, expert_ids, gates, w_in, w_out, out_grad):
    groups = lax.axis_size("expert")
    shards = lax.axis_size("dp")
    token_rows, model_width = tokens.shape
    top_count = expert_ids.shape[1]
    hidden_width = w_out.shape[1]
    capacity = 3 * token_rows * top_count // (2 * groups)
    slots = groups * capacity
    weight_in = w_in[0]
    weight_out = w_out[0]
    ids = expert_ids.T
    gate_rows = gates.T
    named = ids[:, None, :] == jnp.arange(groups, dtype=jnp.int32)[None, :, None]
    member = jnp.any(named, axis=0)
    order = jnp.arange(token_rows, dtype=jnp.int32)
    earlier = (order[:, None] < order[None, :]).astype(jnp.bfloat16)
    rank = jnp.dot(
        member.astype(jnp.bfloat16), earlier, preferred_element_type=jnp.float32
    ).astype(jnp.int32)
    slot_of = jnp.where(member, rank, -1)
    taken = slot_of[:, None, :] == jnp.arange(capacity, dtype=jnp.int32)[None, :, None]
    gate_of = jnp.sum(jnp.where(named, gate_rows[:, None, :], 0.0), axis=0)
    slot_gate = jnp.sum(jnp.where(taken, gate_of[:, None, :], 0.0), axis=2).reshape(slots, 1)
    pick = taken.astype(jnp.bfloat16).reshape(slots, token_rows)

    def exchange(rows):
        return lax.all_to_all(
            rows.reshape(groups, capacity, model_width),
            "expert",
            split_axis=0,
            concat_axis=0,
            tiled=True,
        ).reshape(slots, model_width)

    received = exchange(
        jnp.dot(pick, tokens, preferred_element_type=jnp.float32).astype(jnp.bfloat16)
    )
    grad_rows = exchange(
        (jnp.dot(pick, out_grad, preferred_element_type=jnp.float32) * slot_gate).astype(
            jnp.bfloat16
        )
    )
    gate_up = jnp.dot(received, weight_in, preferred_element_type=jnp.float32)
    gate_part, up_part, hidden = swiglu_forward(gate_up, hidden_width)
    grad_hidden = jnp.dot(grad_rows, weight_out.T, preferred_element_type=jnp.float32)
    grad_gate_up = swiglu_backward(grad_hidden, gate_part, up_part)
    grad_w_in = jnp.dot(received.T, grad_gate_up, preferred_element_type=jnp.float32)
    shard_in = lax.psum_scatter(
        grad_w_in.astype(jnp.bfloat16)[None], "dp", scatter_dimension=1, tiled=True
    )
    grad_w_out = jnp.dot(hidden.T, grad_rows, preferred_element_type=jnp.float32)
    shard_out = halving_sum(
        grad_w_out.reshape(shards, hidden_width // shards, model_width), "dp"
    )[None]
    returned = exchange(
        jnp.dot(hidden, weight_out, preferred_element_type=jnp.float32).astype(jnp.bfloat16)
    )
    grad_back = exchange(
        jnp.dot(grad_gate_up, weight_in.T, preferred_element_type=jnp.float32).astype(
            jnp.bfloat16
        )
    )
    first_slot = jnp.arange(groups, dtype=jnp.int32)[:, None] * capacity
    dest_slot = jnp.sum(jnp.where(named, (first_slot + rank)[None], 0), axis=1)
    home = dest_slot[:, :, None] == jnp.arange(slots, dtype=jnp.int32)[None, None, :]
    per_entry = jnp.dot(
        home.astype(jnp.bfloat16).reshape(top_count * token_rows, slots),
        returned,
        preferred_element_type=jnp.float32,
    ).reshape(top_count, token_rows, model_width)
    upstream = out_grad.astype(jnp.float32)
    mixed = jnp.sum(gate_rows[:, :, None] * per_entry, axis=0).astype(jnp.bfloat16)
    gate_grad = jnp.sum(per_entry * upstream[None], axis=2).T
    token_grad = jnp.dot(
        jnp.any(home, axis=0).astype(jnp.bfloat16), grad_back, preferred_element_type=jnp.float32
    ).astype(jnp.bfloat16)
    return (mixed, token_grad, gate_grad, shard_in, shard_out)


def solution(mesh):
    placed = (
        P(("dp", "expert"), None),
        P(("dp", "expert"), None),
        P(("dp", "expert"), None),
        P("expert", None, None),
        P("expert", None, None),
        P(("dp", "expert"), None),
    )
    return jax.shard_map(
        per_device,
        mesh=mesh,
        in_specs=placed,
        out_specs=(
            P(("dp", "expert"), None),
            P(("dp", "expert"), None),
            P(("dp", "expert"), None),
            P("expert", "dp", None),
            P("expert", "dp", None),
        ),
        check_vma=False,
    )
```

```python
import jax
import jax.numpy as jnp
from jax import lax
from jax.sharding import PartitionSpec as P


def swiglu_forward(gate_up, hidden_width):
    gate_part = gate_up[:, :hidden_width]
    up_part = gate_up[:, hidden_width:]
    return (gate_part, up_part, (jax.nn.silu(gate_part) * up_part).astype(jnp.bfloat16))


def swiglu_backward(grad_hidden, gate_part, up_part):
    sigmoid_gate = jax.nn.sigmoid(gate_part)
    silu_gate = gate_part * sigmoid_gate
    grad_gate = grad_hidden * up_part * (sigmoid_gate * (1.0 + gate_part * (1.0 - sigmoid_gate)))
    grad_up = grad_hidden * silu_gate
    return jnp.concatenate([grad_gate, grad_up], axis=1).astype(jnp.bfloat16)


def halving_sum(parts, axis):
    count = lax.axis_size(axis)
    me = lax.axis_index(axis)
    bit = 1
    while bit < count:
        mine = (me // bit) % 2
        pairs = parts.reshape((parts.shape[0] // 2, 2) + parts.shape[1:])
        keep = lax.dynamic_index_in_dim(pairs, mine, axis=1, keepdims=False)
        send = lax.dynamic_index_in_dim(pairs, 1 - mine, axis=1, keepdims=False)
        came = lax.ppermute(
            send.astype(jnp.bfloat16), axis, [(i, i ^ bit) for i in range(count)]
        )
        parts = keep.astype(jnp.float32) + came.astype(jnp.float32)
        bit *= 2
    return parts[0].astype(jnp.bfloat16)


def per_device(tokens, expert_ids, gates, w_in, w_out, out_grad):
    groups = lax.axis_size("expert")
    shards = lax.axis_size("dp")
    token_rows, model_width = tokens.shape
    top_count = expert_ids.shape[1]
    hidden_width = w_out.shape[1]
    capacity = 3 * token_rows * top_count // (2 * groups)
    slots = groups * capacity
    weight_in = w_in[0]
    weight_out = w_out[0]
    ids = expert_ids.T
    gate_rows = gates.T
    named = ids[:, None, :] == jnp.arange(groups, dtype=jnp.int32)[None, :, None]
    member = jnp.any(named, axis=0)
    order = jnp.arange(token_rows, dtype=jnp.int32)
    earlier = (order[:, None] < order[None, :]).astype(jnp.bfloat16)
    rank = jnp.dot(
        member.astype(jnp.bfloat16), earlier, preferred_element_type=jnp.float32
    ).astype(jnp.int32)
    slot_of = jnp.where(member, rank, -1)
    taken = slot_of[:, None, :] == jnp.arange(capacity, dtype=jnp.int32)[None, :, None]
    gate_of = jnp.sum(jnp.where(named, gate_rows[:, None, :], 0.0), axis=0)
    slot_gate = jnp.sum(jnp.where(taken, gate_of[:, None, :], 0.0), axis=2).reshape(slots, 1)
    pick = taken.astype(jnp.bfloat16).reshape(slots, token_rows)

    def exchange(rows):
        return lax.all_to_all(
            rows.reshape(groups, capacity, model_width),
            "expert",
            split_axis=0,
            concat_axis=0,
            tiled=True,
        ).reshape(slots, model_width)

    received = exchange(
        jnp.dot(pick, tokens, preferred_element_type=jnp.float32).astype(jnp.bfloat16)
    )
    grad_rows = exchange(
        (jnp.dot(pick, out_grad, preferred_element_type=jnp.float32) * slot_gate).astype(
            jnp.bfloat16
        )
    )
    half = shards // 2
    low = lax.axis_index("dp") % 2
    swap = [(i, i ^ 1) for i in range(shards)]
    block = model_width // shards

    def columns(which):
        return jnp.concatenate(
            [
                lax.dynamic_slice_in_dim(received, (2 * h + which) * block, block, axis=1)
                for h in range(half)
            ],
            axis=1,
        )

    grad_rows, other_received = lax.optimization_barrier(
        (grad_rows, lax.ppermute(columns(1 - low), "dp", swap))
    )
    gate_up = jnp.dot(received, weight_in, preferred_element_type=jnp.float32)
    gate_part, up_part, hidden = swiglu_forward(gate_up, hidden_width)
    grad_hidden = jnp.dot(grad_rows, weight_out.T, preferred_element_type=jnp.float32)
    grad_gate_up = swiglu_backward(grad_hidden, gate_part, up_part)
    grad_w_out = jnp.dot(hidden.T, grad_rows, preferred_element_type=jnp.float32)
    other_grad, grad_w_out = lax.optimization_barrier(
        (lax.ppermute(grad_gate_up, "dp", swap), grad_w_out)
    )
    grad_w_in = jnp.dot(columns(low).T, grad_gate_up, preferred_element_type=jnp.float32)
    grad_w_in = grad_w_in + jnp.dot(
        other_received.T, other_grad, preferred_element_type=jnp.float32
    )
    shard_in = lax.psum_scatter(
        grad_w_in.astype(jnp.bfloat16)[None],
        "dp",
        scatter_dimension=1,
        axis_index_groups=[[2 * h + b for h in range(half)] for b in range(2)],
        tiled=True,
    )
    shard_out = halving_sum(
        grad_w_out.reshape(shards, hidden_width // shards, model_width), "dp"
    )[None]
    returned = exchange(
        jnp.dot(hidden, weight_out, preferred_element_type=jnp.float32).astype(jnp.bfloat16)
    )
    grad_back = exchange(
        jnp.dot(grad_gate_up, weight_in.T, preferred_element_type=jnp.float32).astype(
            jnp.bfloat16
        )
    )
    first_slot = jnp.arange(groups, dtype=jnp.int32)[:, None] * capacity
    dest_slot = jnp.sum(jnp.where(named, (first_slot + rank)[None], 0), axis=1)
    home = dest_slot[:, :, None] == jnp.arange(slots, dtype=jnp.int32)[None, None, :]
    per_entry = jnp.dot(
        home.astype(jnp.bfloat16).reshape(top_count * token_rows, slots),
        returned,
        preferred_element_type=jnp.float32,
    ).reshape(top_count, token_rows, model_width)
    upstream = out_grad.astype(jnp.float32)
    mixed = jnp.sum(gate_rows[:, :, None] * per_entry, axis=0).astype(jnp.bfloat16)
    gate_grad = jnp.sum(per_entry * upstream[None], axis=2).T
    token_grad = jnp.dot(
        jnp.any(home, axis=0).astype(jnp.bfloat16), grad_back, preferred_element_type=jnp.float32
    ).astype(jnp.bfloat16)
    return (mixed, token_grad, gate_grad, shard_in, shard_out)


def solution(mesh):
    placed = (
        P(("dp", "expert"), None),
        P(("dp", "expert"), None),
        P(("dp", "expert"), None),
        P("expert", None, None),
        P("expert", None, None),
        P(("dp", "expert"), None),
    )
    return jax.shard_map(
        per_device,
        mesh=mesh,
        in_specs=placed,
        out_specs=(
            P(("dp", "expert"), None),
            P(("dp", "expert"), None),
            P(("dp", "expert"), None),
            P("expert", "dp", None),
            P("expert", "dp", None),
        ),
        check_vma=False,
    )
```

```python
import jax
import jax.numpy as jnp
from jax import lax
from jax.sharding import PartitionSpec as P


def swiglu_forward(gate_up, hidden_width):
    gate_part = gate_up[:, :hidden_width]
    up_part = gate_up[:, hidden_width:]
    return (gate_part, up_part, (jax.nn.silu(gate_part) * up_part).astype(jnp.bfloat16))


def swiglu_backward(grad_hidden, gate_part, up_part):
    sigmoid_gate = jax.nn.sigmoid(gate_part)
    silu_gate = gate_part * sigmoid_gate
    grad_gate = grad_hidden * up_part * (sigmoid_gate * (1.0 + gate_part * (1.0 - sigmoid_gate)))
    grad_up = grad_hidden * silu_gate
    return jnp.concatenate([grad_gate, grad_up], axis=1).astype(jnp.bfloat16)


def halving_sum(parts, axis, beside):
    count = lax.axis_size(axis)
    me = lax.axis_index(axis)
    bits = [1 << i for i in range(count.bit_length() - 1)]
    left = list(bits)
    for bit in bits[1:2] + bits[:1] + bits[2:]:
        mine = (me // bit) % 2
        below = 1 << left.index(bit)

        def side(x, which):
            x = x.reshape((x.shape[0] // (2 * below), 2, below) + x.shape[1:])
            x = lax.dynamic_index_in_dim(x, which, axis=1, keepdims=False)
            return x.reshape((x.shape[0] * below,) + x.shape[2:])

        send = side(parts, 1 - mine).astype(jnp.bfloat16)
        if len(left) == len(bits):
            send, beside = lax.optimization_barrier((send, beside))
        came = lax.ppermute(send, axis, [(i, i ^ bit) for i in range(count)])
        parts = side(parts, mine).astype(jnp.float32) + came.astype(jnp.float32)
        left.remove(bit)
    return parts[0].astype(jnp.bfloat16), beside


def per_device(tokens, expert_ids, gates, w_in, w_out, out_grad):
    groups = lax.axis_size("expert")
    shards = lax.axis_size("dp")
    token_rows, model_width = tokens.shape
    top_count = expert_ids.shape[1]
    hidden_width = w_out.shape[1]
    capacity = 3 * token_rows * top_count // (2 * groups)
    slots = groups * capacity
    weight_in = w_in[0]
    weight_out = w_out[0]
    ids = expert_ids.T
    gate_rows = gates.T
    named = ids[:, None, :] == jnp.arange(groups, dtype=jnp.int32)[None, :, None]
    member = jnp.any(named, axis=0)
    order = jnp.arange(token_rows, dtype=jnp.int32)
    earlier = (order[:, None] < order[None, :]).astype(jnp.bfloat16)
    rank = jnp.dot(
        member.astype(jnp.bfloat16), earlier, preferred_element_type=jnp.float32
    ).astype(jnp.int32)
    slot_of = jnp.where(member, rank, -1)
    taken = slot_of[:, None, :] == jnp.arange(capacity, dtype=jnp.int32)[None, :, None]
    gate_of = jnp.sum(jnp.where(named, gate_rows[:, None, :], 0.0), axis=0)
    slot_gate = jnp.sum(jnp.where(taken, gate_of[:, None, :], 0.0), axis=2).reshape(slots, 1)
    pick = taken.astype(jnp.bfloat16).reshape(slots, token_rows)

    def exchange(rows):
        return lax.all_to_all(
            rows.reshape(groups, capacity, model_width),
            "expert",
            split_axis=0,
            concat_axis=0,
            tiled=True,
        ).reshape(slots, model_width)

    received = exchange(
        jnp.dot(pick, tokens, preferred_element_type=jnp.float32).astype(jnp.bfloat16)
    )
    grad_rows = exchange(
        (jnp.dot(pick, out_grad, preferred_element_type=jnp.float32) * slot_gate).astype(
            jnp.bfloat16
        )
    )
    half = shards // 2
    low = lax.axis_index("dp") % 2
    swap = [(i, i ^ 1) for i in range(shards)]
    block = model_width // shards

    def columns(which):
        return jnp.concatenate(
            [
                lax.dynamic_slice_in_dim(received, (2 * h + which) * block, block, axis=1)
                for h in range(half)
            ],
            axis=1,
        )

    grad_rows, other_received = lax.optimization_barrier(
        (grad_rows, lax.ppermute(columns(1 - low), "dp", swap))
    )
    gate_up = jnp.dot(received, weight_in, preferred_element_type=jnp.float32)
    gate_part, up_part, hidden = swiglu_forward(gate_up, hidden_width)
    grad_hidden = jnp.dot(grad_rows, weight_out.T, preferred_element_type=jnp.float32)
    grad_gate_up = swiglu_backward(grad_hidden, gate_part, up_part)
    grad_w_out = jnp.dot(hidden.T, grad_rows, preferred_element_type=jnp.float32)
    by_shard = (shards, hidden_width // shards, model_width)
    other_gate = lax.ppermute(grad_gate_up[:, :hidden_width], "dp", swap)
    shard_out, up_half = halving_sum(
        grad_w_out.reshape(by_shard), "dp", grad_gate_up[:, hidden_width:]
    )
    other_grad = jnp.concatenate([other_gate, lax.ppermute(up_half, "dp", swap)], axis=1)
    grad_w_in = jnp.dot(columns(low).T, grad_gate_up, preferred_element_type=jnp.float32)
    grad_w_in = grad_w_in + jnp.dot(
        other_received.T, other_grad, preferred_element_type=jnp.float32
    )
    shard_in = lax.psum_scatter(
        grad_w_in.astype(jnp.bfloat16)[None],
        "dp",
        scatter_dimension=1,
        axis_index_groups=[[2 * h + b for h in range(half)] for b in range(2)],
        tiled=True,
    )
    returned = exchange(
        jnp.dot(hidden, weight_out, preferred_element_type=jnp.float32).astype(jnp.bfloat16)
    )
    grad_back = exchange(
        jnp.dot(grad_gate_up, weight_in.T, preferred_element_type=jnp.float32).astype(
            jnp.bfloat16
        )
    )
    first_slot = jnp.arange(groups, dtype=jnp.int32)[:, None] * capacity
    dest_slot = jnp.sum(jnp.where(named, (first_slot + rank)[None], 0), axis=1)
    home = dest_slot[:, :, None] == jnp.arange(slots, dtype=jnp.int32)[None, None, :]
    per_entry = jnp.dot(
        home.astype(jnp.bfloat16).reshape(top_count * token_rows, slots),
        returned,
        preferred_element_type=jnp.float32,
    ).reshape(top_count, token_rows, model_width)
    upstream = out_grad.astype(jnp.float32)
    mixed = jnp.sum(gate_rows[:, :, None] * per_entry, axis=0).astype(jnp.bfloat16)
    gate_grad = jnp.sum(per_entry * upstream[None], axis=2).T
    token_grad = jnp.dot(
        jnp.any(home, axis=0).astype(jnp.bfloat16), grad_back, preferred_element_type=jnp.float32
    ).astype(jnp.bfloat16)
    return (mixed, token_grad, gate_grad, shard_in, shard_out[None])


def solution(mesh):
    placed = (
        P(("dp", "expert"), None),
        P(("dp", "expert"), None),
        P(("dp", "expert"), None),
        P("expert", None, None),
        P("expert", None, None),
        P(("dp", "expert"), None),
    )
    return jax.shard_map(
        per_device,
        mesh=mesh,
        in_specs=placed,
        out_specs=(
            P(("dp", "expert"), None),
            P(("dp", "expert"), None),
            P(("dp", "expert"), None),
            P("expert", "dp", None),
            P("expert", "dp", None),
        ),
        check_vma=False,
    )
```
